32 devices in a mesh: grp: 2 (over y), pb: 4 (over z), ha: 4 (over x, core).
Axes of the slice: x: 2, y: 2, z: 4, core: 2. Of those that a mesh axis runs over, the one named last changes fastest.
Arguments:
- latents: bfloat16 [8, 384, 3072], P(('grp', 'pb'), None, 'ha'), parts along dimension 0, may hold values from -6 to 6
- timesteps: int32 [8], P(('grp', 'pb')), parts along dimension 0, may hold values from 0 to 999
- mod_weight: bfloat16 [256, 3, 3072], P(None, None, 'ha'), may hold values from -0.375 to 0.375
- qkv_weight: bfloat16 [3072, 3, 3072], P(None, None, 'ha'), may hold values from -0.109375 to 0.109375
- out_weight: bfloat16 [3072, 3072], P('ha'), may hold values from -0.15625 to 0.15625
- noise_frame: bfloat16 [768, 3072], P('grp', 'ha'), parts along dimension 0, may hold values from -6 to 6
Outputs:
- advanced: bfloat16 [8, 384, 3072], P(('grp', 'pb'), None, 'ha'), parts along dimension 0
- queue_next: bfloat16 [8, 384, 3072], P(('grp', 'pb'), None, 'ha'), parts along dimension 0
The draws below stay inside these ranges and needn't reach their ends.
There are 2 independent parts, one for each index of `grp`. The reference program is written for one: setup_inputs(seed, part) draws one part's arguments, and reference() takes and returns one part's arrays. A program takes and returns all parts, laid end to end along the dimension named above; an argument that names none is the same for every part. Nothing has to cross between parts.
All inputs are finite; a program needn't handle non-finite values.
Results may differ from the reference program's by a relative error of at most 0.0045.
Values may be sent and summed in bfloat16 or wider, within the bound.
No kernel may reach another device: no remote copies, remote signals or barrier semaphores. Data moves between devices by JAX's collectives and lax.ppermute only.
A program may use at most 64 MiB of HBM per device.

```python
import math
import jax
import jax.numpy as jnp
from jax import lax

D = 3072
HEADS = 24
HD = 128
TDIM = 256
TOK_F = 384
FRAMES = 4


def draw_latents(key, part):
    noise_key = jax.random.fold_in(key, 11)
    direction_key = jax.random.fold_in(key, 12)
    sign_key = jax.random.fold_in(key, 13)
    noise_part = jax.random.normal(noise_key, (FRAMES, TOK_F, D), jnp.float32)
    direction = jax.random.normal(direction_key, (FRAMES, 1, D), jnp.float32)
    token_signs = (2 * jax.random.randint(sign_key, (FRAMES, TOK_F, 1), 0, 2) - 1).astype(jnp.float32)
    values = 0.71 * (noise_part + token_signs * direction)
    return jnp.clip(values, -6.0, 6.0).astype(jnp.bfloat16)


def set_ends(entries, rng, smallest, top_value):
    longest = entries.shape.index(max(entries.shape))
    spots = []
    for shift in (0, 1):
        where = [jax.random.randint(jax.random.fold_in(rng, axis), (), 0, length) for axis, length in enumerate(entries.shape)]
        where[longest] = (where[longest] + shift) % entries.shape[longest]
        spots.append(tuple(where))
    return entries.at[spots[0]].set(smallest).at[spots[1]].set(top_value)


def raised(result, stream_key, source, target, shards_of, factor):
    def block_of(dim):
        return (jnp.arange(result.shape[dim]) // (result.shape[dim] // shards_of)).reshape((-1,) + (1,) * (result.ndim - 1 - dim))

    one_side = jax.random.permutation(stream_key, shards_of)[block_of(target)]
    far = (block_of(target) + shards_of // 2) % shards_of
    return jnp.where((block_of(source) == one_side) | (block_of(source) == far), factor * result, result)


def steps_of(key, dims, shards, low, high):
    gain = 1.0
    for position, blocks in shards:
        draws = jax.random.uniform(jax.random.fold_in(jax.random.fold_in(key, 6), position), (blocks,), jnp.float32, low / len(shards), high / len(shards))
        gain = gain * jnp.repeat(jnp.exp(draws), dims[position] // blocks).reshape((-1,) + (1,) * (len(dims) - 1 - position))
    return gain


def gaussian(rng, shape, spread, limit, pieces=(), kind=jnp.bfloat16):
    entries = jax.random.normal(rng, shape, jnp.float32) * spread
    if len(pieces) > 0:
        entries = steps_of(rng, shape, pieces, -0.22, 0.18) * entries
    return jnp.clip(entries, min=-limit, max=limit).astype(kind)


def gaussian_with(own_key, dims, deviation, limit, pieces, heavy, kind=jnp.bfloat16):
    entries = deviation * jax.random.normal(own_key, dims, jnp.float32)
    if pieces:
        entries = entries * steps_of(own_key, dims, pieces, -0.22, 0.18)
    return jnp.clip(raised(entries, jax.random.fold_in(own_key, 3), *heavy), -limit, limit).astype(kind)


def setup_inputs(seed: int = 0, part: int = 0) -> dict:
    key_list = jax.random.split(jax.random.key(seed), 7)
    part_splits = jax.random.split(jax.random.fold_in(key_list[6], part), 7)
    return {
        "latents": draw_latents(jax.random.fold_in(jax.random.fold_in(key_list[6], part), 71), part),
        "timesteps": set_ends(jax.random.randint(part_splits[1], (FRAMES,), 0, 1000), jax.random.fold_in(part_splits[1], 1), 0, 999).astype(jnp.int32),
        "mod_weight": gaussian(key_list[2], (TDIM, 3, D), TDIM ** -0.5, 0.375, ((2, 4),)),
        "qkv_weight": gaussian(key_list[3], (D, 3, D), D ** -0.5, 0.109375, ((2, 4),)),
        "out_weight": gaussian_with(key_list[4], (D, D), D ** -0.5, 0.15625, ((0, 4),), (0, 1, 4, 2.0)),
        "noise_frame": gaussian(part_splits[5], (TOK_F, D), 1.0, 6.0, ((1, 4),)),
    }


def sinusoid(timesteps):
    half_width = TDIM // 2
    frequency = jnp.exp(-math.log(10000.0) * jnp.arange(half_width, dtype=jnp.float32) / half_width)
    angles = timesteps.astype(jnp.float32)[:, None] * frequency[None, :]
    return jnp.concatenate([jnp.cos(angles), jnp.sin(angles)], axis=1)

def unit_rms(vectors):
    return vectors * lax.rsqrt(lax.optimization_barrier(jnp.mean(vectors * vectors, axis=-1, keepdims=True)) + 1e-06)

def reference(latents, timesteps, mod_weight, qkv_weight, out_weight, noise_frame):
    frames = latents.shape[0]
    embedding = sinusoid(timesteps).astype(jnp.bfloat16)
    modulation = jnp.dot(embedding, mod_weight.reshape(TDIM, 3 * D), preferred_element_type=jnp.float32)
    modulation = modulation.astype(jnp.bfloat16).reshape(frames, 3, D).astype(jnp.float32)
    latent_wide = latents.astype(jnp.float32)
    row_mean = lax.optimization_barrier(jnp.mean(latent_wide, axis=-1, keepdims=True))
    centered = latent_wide - row_mean
    row_var = lax.optimization_barrier(jnp.mean(centered * centered, axis=-1, keepdims=True))
    normed = centered * lax.rsqrt(row_var + 1e-06)
    hidden = normed * (1.0 + modulation[:, 1][:, None, :]) + modulation[:, 0][:, None, :]
    hidden = hidden.astype(jnp.bfloat16).reshape(frames * TOK_F, D)
    projected = jnp.dot(hidden, qkv_weight.reshape(D, 3 * D), preferred_element_type=jnp.float32)
    projected = projected.reshape(frames * TOK_F, 3, HEADS, HD)
    queries = (unit_rms(projected[:, 0]) / math.sqrt(HD)).astype(jnp.bfloat16)
    key_rows = unit_rms(projected[:, 1]).astype(jnp.bfloat16).astype(jnp.float32)
    value_rows = projected[:, 2].astype(jnp.bfloat16).astype(jnp.float32)

    def attend_frame(query_frame):
        scores = jnp.einsum('qhd,khd->hqk', query_frame.astype(jnp.float32), key_rows)
        weights_exp = jnp.exp(scores)
        denominator = lax.optimization_barrier(jnp.sum(weights_exp, axis=2))
        numerator = jnp.einsum('hqk,khd->qhd', weights_exp.astype(jnp.bfloat16).astype(jnp.float32), value_rows)
        return (numerator / denominator.T[:, :, None]).astype(jnp.bfloat16)
    attended = lax.map(attend_frame, queries.reshape(frames, TOK_F, HEADS, HD))
    attended = attended.reshape(frames * TOK_F, D)
    branch = jnp.dot(attended, out_weight, preferred_element_type=jnp.float32).reshape(frames, TOK_F, D)
    advanced = (latent_wide + modulation[:, 2][:, None, :] * branch).astype(jnp.bfloat16)
    queue_next = jnp.concatenate([advanced[1:], noise_frame[None]], axis=0)
    return (advanced, queue_next)
```

```python
import functools
import math

import jax
import jax.numpy as jnp
from jax import lax
from jax.experimental import pallas as pl
from jax.experimental.pallas import tpu as pltpu
from jax.sharding import PartitionSpec as P

HD = 128
TDIM = 256
F32 = jnp.float32
BF16 = jnp.bfloat16
VMEM_LIMIT = 40 * 1024 * 1024


def flip(x, axis, bit):
    size = lax.axis_size(axis)
    return lax.ppermute(x, axis, [(i, i ^ bit) for i in range(size)])


def from_behind(x, axis, by):
    size = lax.axis_size(axis)
    pairs = [(i, i + by) for i in range(size) if 0 <= i + by < size]
    return lax.ppermute(x, axis, pairs)


def sinusoid(timesteps):
    half_width = TDIM // 2
    frequency = jnp.exp(-math.log(10000.0) * jnp.arange(half_width, dtype=F32) / half_width)
    angles = timesteps.astype(F32)[:, None] * frequency[None, :]
    return jnp.concatenate([jnp.cos(angles), jnp.sin(angles)], axis=1)


def unit_rms(vectors):
    return vectors * lax.rsqrt(jnp.mean(vectors * vectors, axis=-1, keepdims=True) + 1e-06)


def norm_rows(ids_ref, piece_refs, mod_ref, hidden_ref):
    ha, frame = ids_ref[0], ids_ref[1]
    count = len(piece_refs)
    rows, width = piece_refs[0].shape
    step = 16

    def one(i, carry):
        at = pl.ds(pl.multiple_of(i * step, step), step)
        wide = [ref[at, :].astype(F32) for ref in piece_refs]
        total = sum(jnp.sum(w, axis=-1, keepdims=True) for w in wide)
        mean = total / (count * width)
        wide = [w - mean for w in wide]
        square = sum(jnp.sum(w * w, axis=-1, keepdims=True) for w in wide)
        inverse = lax.rsqrt(square / (count * width) + 1e-06)
        for j in range(count):
            block = lax.bitwise_xor(ha, j)
            mod = mod_ref[frame * count + block]
            out = wide[j] * inverse * (1.0 + mod[1:2]) + mod[0:1]
            hidden_ref[at, pl.ds(pl.multiple_of(block * width, HD), width)] = out.astype(BF16)
        return carry

    lax.fori_loop(0, rows // step, one, 0, unroll=2)


def attend(q, k, v, num, den):
    scores = lax.dot_general(q, k, (((1,), (1,)), ((), ())), preferred_element_type=F32)
    weights = jnp.exp(scores)
    for start in range(0, weights.shape[1], HD):
        part = weights[:, start : start + HD]
        den = part if den is None else den + part
    more = jnp.dot(weights.astype(BF16), v, preferred_element_type=F32)
    return more if num is None else num + more, den


def frame_body(own, last, count, heads, ids_ref, *refs):
    pieces, refs = refs[:count], refs[count:]
    mod_ref, refs = refs[0], refs[1:]
    if own:
        wq_ref, wk_ref, wv_ref, q_out, num_out, den_out, hidden_ref = refs
    elif last:
        wk_ref, wv_ref, q_ref, num_ref, den_ref, att_out, hidden_ref = refs
    else:
        wk_ref, wv_ref, q_ref, num_ref, den_ref, num_out, den_out, hidden_ref = refs

    @pl.when(pl.program_id(0) == 0)
    def _():
        norm_rows(ids_ref, pieces, mod_ref, hidden_ref)

    hidden = hidden_ref[...]
    key_all = jnp.dot(hidden, wk_ref[0], preferred_element_type=F32)
    value_all = jnp.dot(hidden, wv_ref[0], preferred_element_type=F32)
    query_all = jnp.dot(hidden, wq_ref[0], preferred_element_type=F32) if own else None
    for head in range(heads):
        at = slice(head * HD, (head + 1) * HD)
        k = unit_rms(key_all[:, at]).astype(BF16)
        v = value_all[:, at].astype(BF16)
        if own:
            q = (unit_rms(query_all[:, at]) * (1.0 / math.sqrt(HD))).astype(BF16)
            q_out[:, at] = q
            num, den = attend(q, k, v, None, None)
        else:
            num, den = attend(q_ref[:, at], k, v, num_ref[:, at], den_ref[:, at])
        if last:
            att_out[:, at] = (num / jnp.sum(den, axis=-1, keepdims=True)).astype(BF16)
        else:
            num_out[:, at] = num
            den_out[:, at] = den


def frame_step(ids, pieces, mods, weight, state, last):
    own = state is None
    count = len(pieces)
    rows, width = pieces[0].shape
    full = weight.shape[1]
    head_local = width // HD
    heads = 2 if head_local % 2 == 0 else 1
    block = heads * HD
    weight_at = lambda j: pl.BlockSpec((1, full, block), lambda h, ids: (j, 0, h))
    whole = pl.BlockSpec((rows, width), lambda h, ids: (0, 0))
    queries = rows if own else state[0].shape[0]
    column = pl.BlockSpec((queries, block), lambda h, ids: (0, h))
    in_specs = [whole] * count + [pl.BlockSpec(mods.shape, lambda h, ids: (0, 0, 0))]
    args = [ids, *pieces, mods]
    used = (0, 1, 2) if own else (1, 2)
    in_specs += [weight_at(j) for j in used]
    args += [weight] * len(used)
    wide = jax.ShapeDtypeStruct((queries, width), F32)
    thin = jax.ShapeDtypeStruct((queries, width), BF16)
    if own:
        outs = (thin, wide, wide)
    else:
        in_specs += [column] * 3
        args += state
        outs = (thin,) if last else (wide, wide)
    flops = 2 * rows * full * width * len(used) + 4 * queries * rows * width
    return pl.pallas_call(
        functools.partial(frame_body, own, last, count, heads),
        grid_spec=pltpu.PrefetchScalarGridSpec(
            num_scalar_prefetch=1,
            grid=(head_local // heads,),
            in_specs=in_specs,
            out_specs=tuple(column for _ in outs),
            scratch_shapes=[pltpu.VMEM((rows, full), BF16)],
        ),
        out_shape=outs,
        compiler_params=pltpu.CompilerParams(vmem_limit_bytes=VMEM_LIMIT),
        cost_estimate=pl.CostEstimate(
            flops=flops, bytes_accessed=2 * full * width * len(used), transcendentals=queries * rows * head_local
        ),
    )(*args)


def project_body(ids_ref, *refs):
    *ins, out_ref = refs
    half = len(ins) // 2
    total = None
    for att_ref, weight_ref in zip(ins[:half], ins[half:]):
        part = jnp.dot(att_ref[...], weight_ref[...], preferred_element_type=F32)
        total = part if total is None else total + part
    out_ref[...] = total.astype(out_ref.dtype)


def project(ids, attended, weights, index_maps, dtype):
    rows, width = attended[0].shape
    flops = 2 * rows * width * width * len(attended)
    return pl.pallas_call(
        project_body,
        grid_spec=pltpu.PrefetchScalarGridSpec(
            num_scalar_prefetch=1,
            grid=(1,),
            in_specs=[pl.BlockSpec((rows, width), lambda i, ids: (0, 0)) for _ in attended]
            + [pl.BlockSpec((width, width), index_map) for index_map in index_maps],
            out_specs=pl.BlockSpec((rows, width), lambda i, ids: (0, 0)),
        ),
        out_shape=jax.ShapeDtypeStruct((rows, width), dtype),
        compiler_params=pltpu.CompilerParams(vmem_limit_bytes=VMEM_LIMIT),
        cost_estimate=pl.CostEstimate(
            flops=flops, bytes_accessed=2 * width * width * len(attended), transcendentals=0
        ),
    )(ids, *attended, *weights)


def spread(piece):
    size = lax.axis_size("ha")
    out = [None] * size
    out[0] = piece
    for step in range(2, size, 2):
        out[step] = flip(piece, "ha", step)
    for step in range(0, size, 2):
        out[step + 1] = flip(out[step], "ha", 1)
    return out


def on_device(latents, timesteps, mod_weight, qkv_weight, out_weight, noise_frame):
    frames, tok_count, width = latents.shape
    ha_size, pb_size = lax.axis_size("ha"), lax.axis_size("pb")
    ha, pb = lax.axis_index("ha"), lax.axis_index("pb")
    piece = latents.reshape(tok_count, width)
    weight = jnp.transpose(qkv_weight, (1, 0, 2))

    embedding = sinusoid(timesteps).astype(BF16)
    modulation = jnp.einsum(
        "pe,jef->pjf", embedding, jnp.transpose(mod_weight, (1, 0, 2)), preferred_element_type=F32
    ).astype(BF16)
    mods = lax.all_gather(modulation[:, :2], ("pb", "ha"), axis=0, tiled=True).astype(F32)
    gate = modulation[:, 2].astype(F32)

    columns = [
        lax.dynamic_slice_in_dim(out_weight, lax.bitwise_xor(ha, step + 1) * width, width, 1)
        for step in range(0, ha_size, 2)
    ]
    other_weight = [flip(c, "ha", 1) for c in columns]

    def ids_of(bit):
        return jnp.stack([ha, lax.bitwise_xor(pb, bit)]).astype(jnp.int32)

    own_pieces = spread(piece)
    order = list(range(1, pb_size))
    arrived = []
    for n, bit in enumerate(order):
        if n == len(order) - 1 and tok_count == 384:
            arrived.append((bit, flip(piece[:256], "pb", bit)))
            arrived.append((bit, flip(piece[256:], "pb", bit)))
        else:
            arrived.append((bit, flip(piece, "pb", bit)))
    q, num, den = frame_step(ids_of(0), own_pieces, mods, weight, None, False)
    for n, (bit, got) in enumerate(arrived):
        last = n == len(arrived) - 1
        result = frame_step(ids_of(bit), spread(got), mods, weight, (q, num, den), last)
        if last:
            (attended,) = result
        else:
            num, den = result

    ids = ids_of(0)
    is_last = pb == pb_size - 1
    done, following = [], []
    for start, stop in ((0, tok_count // 2), (tok_count // 2, tok_count)):
        mine = attended[start:stop]
        both = (mine, flip(mine, "ha", 1))
        branch = None
        for step in range(ha_size - 2, -1, -2):
            at = lambda i, ids, step=step: (0, lax.bitwise_xor(ids[0], step))
            zero = lambda i, ids: (0, 0)
            part = project(
                ids, both, (out_weight, other_weight[step // 2]), (at, zero), BF16 if step else F32
            )
            if step:
                part = flip(part, "ha", step).astype(F32)
            branch = part if branch is None else branch + part
        advanced = (piece[start:stop].astype(F32) + gate * branch).astype(BF16)
        incoming = from_behind(advanced, "pb", -1)
        done.append(advanced)
        following.append(jnp.where(is_last, noise_frame[start:stop], incoming))
    return jnp.concatenate(done, axis=0)[None], jnp.concatenate(following, axis=0)[None]


def solution(mesh):
    placed = (
        P(("grp", "pb"), None, "ha"),
        P(("grp", "pb")),
        P(None, None, "ha"),
        P(None, None, "ha"),
        P("ha", None),
        P("grp", "ha"),
    )
    return jax.shard_map(
        on_device,
        mesh=mesh,
        in_specs=placed,
        out_specs=(P(("grp", "pb"), None, "ha"), P(("grp", "pb"), None, "ha")),
        check_vma=False,
    )
```

```python
import functools
import math

import jax
import jax.numpy as jnp
from jax import lax
from jax.experimental import pallas as pl
from jax.experimental.pallas import tpu as pltpu
from jax.sharding import PartitionSpec as P

HD = 128
TDIM = 256
F32 = jnp.float32
BF16 = jnp.bfloat16
VMEM_LIMIT = 20 * 1024 * 1024
MOD_ROWS = 16


def flip(x, axis, bit):
    size = lax.axis_size(axis)
    return lax.ppermute(x, axis, [(i, i ^ bit) for i in range(size)])


def from_behind(x, axis, by):
    size = lax.axis_size(axis)
    pairs = [(i, i + by) for i in range(size) if 0 <= i + by < size]
    return lax.ppermute(x, axis, pairs)


def sinusoid(timesteps):
    half_width = TDIM // 2
    frequency = jnp.exp(-math.log(10000.0) * jnp.arange(half_width, dtype=F32) / half_width)
    angles = timesteps.astype(F32)[:, None] * frequency[None, :]
    return jnp.concatenate([jnp.cos(angles), jnp.sin(angles)], axis=1)


def unit_rms(vectors):
    return vectors * lax.rsqrt(jnp.mean(vectors * vectors, axis=-1, keepdims=True) + 1e-06)


def norm_rows(ha, piece_refs, mod_refs, offset, hidden_ref, scale_ref, shift_ref):
    count = len(piece_refs)
    rows, full = hidden_ref.shape
    width = full // count
    step = 64
    spots = []
    for j in range(count):
        spot = pl.ds(pl.multiple_of(lax.bitwise_xor(ha, j) * width, HD), width)
        mod = mod_refs[j][0:MOD_ROWS, :].astype(F32)
        shift_ref[j] = jnp.broadcast_to(mod[0:1], (8, width))
        scale_ref[j] = jnp.broadcast_to(1.0 + mod[1:2], (8, width))
        spots.append(spot)

    def one(i, carry):
        at = pl.ds(pl.multiple_of(offset + i * step, 16), step)
        to = pl.ds(pl.multiple_of(i * step, step), step)

        def sum_rows(parts):
            total = None
            for part in parts:
                for k in range(0, width, HD):
                    tile = part[:, k : k + HD]
                    total = tile if total is None else total + tile
            return jnp.sum(total, axis=-1, keepdims=True) * (1.0 / full)

        mean = sum_rows(ref[at, :].astype(F32) for ref in piece_refs)
        inverse = lax.rsqrt(sum_rows(jnp.square(ref[at, :].astype(F32) - mean) for ref in piece_refs) + 1e-06)
        for j, ref in enumerate(piece_refs):
            normed = ((ref[at, :].astype(F32) - mean) * inverse).reshape(step // 8, 8, width)
            out = normed * scale_ref[j][None] + shift_ref[j][None]
            hidden_ref[to, spots[j]] = out.reshape(step, width).astype(BF16)
        return carry

    lax.fori_loop(0, rows // step, one, 0)


def attend(q, k, v, num, den):
    scores = lax.dot_general(q, k, (((1,), (1,)), ((), ())), preferred_element_type=F32)
    weights = jnp.exp(scores)
    for start in range(0, weights.shape[1], HD):
        part = weights[:, start : start + HD]
        if part.shape[1] < HD:
            part = jnp.concatenate([part, jnp.zeros((part.shape[0], HD - part.shape[1]), F32)], axis=1)
        den = part if den is None else den + part
    more = jnp.dot(weights.astype(BF16), v, preferred_element_type=F32)
    return more if num is None else num + more, den


def frame_body(own, last, count, offset, separate, ids_ref, *refs):
    refs = list(refs)
    pieces, refs = refs[:count], refs[count:]
    mods = pieces
    if separate:
        mods, refs = refs[:count], refs[count:]
    weight_ref, refs = refs[0], refs[1:]
    hidden_ref, scale_ref, shift_ref = refs[-3:]
    if own:
        q_out, num_out, den_out = refs[:-3]
    elif last:
        q_ref, num_ref, den_ref, att_out = refs[:-3]
    else:
        q_ref, num_ref, den_ref, num_out, den_out = refs[:-3]
    norm_rows(ids_ref[0], pieces, mods, offset, hidden_ref, scale_ref, shift_ref)
    width = weight_ref.shape[2]
    block = 2 * HD if width % (2 * HD) == 0 else HD
    for start in range(0, width, block):
        hidden = hidden_ref[...]
        columns = slice(start, start + block)
        key_all = jnp.dot(hidden, weight_ref[1, :, columns], preferred_element_type=F32)
        value_all = jnp.dot(hidden, weight_ref[2, :, columns], preferred_element_type=F32)
        query_all = jnp.dot(hidden, weight_ref[0, :, columns], preferred_element_type=F32) if own else None
        for head in range(0, block, HD):
            inner = slice(head, head + HD)
            at = slice(start + head, start + head + HD)
            k = unit_rms(key_all[:, inner]).astype(BF16)
            v = value_all[:, inner].astype(BF16)
            if own:
                q = (unit_rms(query_all[:, inner]) * (1.0 / math.sqrt(HD))).astype(BF16)
                q_out[:, at] = q
                num, den = attend(q, k, v, None, None)
            else:
                num, den = attend(q_ref[:, at], k, v, num_ref[:, at], den_ref[:, at])
            if last:
                att_out[:, at] = (num / jnp.sum(den, axis=-1, keepdims=True)).astype(BF16)
            else:
                num_out[:, at] = num
                den_out[:, at] = den


def frame_step(ids, pieces, mods, weight, state, last=False, offset=0):
    own = state is None
    count = len(pieces)
    width = pieces[0].shape[1]
    rows = pieces[0].shape[0] - offset
    full = weight.shape[1]
    queries = rows if own else state[0].shape[0]
    args = [*pieces, *(mods or ()), weight, *(state or ())]
    wide = jax.ShapeDtypeStruct((queries, width), F32)
    thin = jax.ShapeDtypeStruct((queries, width), BF16)
    outs = (thin, wide, wide) if own else (thin,) if last else (wide, wide)
    used = 3 if own else 2
    args = [pltpu.with_memory_space_constraint(x, pltpu.VMEM) if x is weight else x for x in args]
    vmem = pl.BlockSpec(memory_space=pltpu.VMEM)
    return pl.pallas_call(
        functools.partial(frame_body, own, last, count, offset, mods is not None),
        in_specs=[pl.BlockSpec(memory_space=pltpu.SMEM)] + [vmem] * len(args),
        out_specs=tuple(vmem for _ in outs),
        scratch_shapes=[
            pltpu.VMEM((rows, full), BF16),
            pltpu.VMEM((count, 8, width), F32),
            pltpu.VMEM((count, 8, width), F32),
        ],
        out_shape=outs,
        compiler_params=pltpu.CompilerParams(vmem_limit_bytes=VMEM_LIMIT),
        cost_estimate=pl.CostEstimate(
            flops=rows * full * width // 8, bytes_accessed=rows * full // 8, transcendentals=0
        ),
    )(ids, *args)


def fetch_body(ids_ref, weight_ref, out_ref, weight_out, out_out, *rest):
    *column_outs, sems = rest
    width = out_ref.shape[0]
    copies = [
        pltpu.make_async_copy(weight_ref, weight_out, sems.at[0]),
        pltpu.make_async_copy(out_ref, out_out, sems.at[1]),
    ]
    for n, column_out in enumerate(column_outs):
        at = pl.ds(pl.multiple_of(lax.bitwise_xor(ids_ref[0], 2 * n + 1) * width, HD), width)
        copies.append(pltpu.make_async_copy(out_ref.at[:, at], column_out, sems.at[n + 2]))
    for copy in copies:
        copy.start()
    for copy in copies:
        copy.wait()


def fetch(ids, weight, out_weight, ha_size):
    width = out_weight.shape[0]
    columns = ha_size // 2
    anywhere, vmem = pl.BlockSpec(memory_space=pltpu.HBM), pl.BlockSpec(memory_space=pltpu.VMEM)
    return pl.pallas_call(
        fetch_body,
        in_specs=[pl.BlockSpec(memory_space=pltpu.SMEM), anywhere, anywhere],
        out_specs=(vmem, vmem) + (anywhere,) * columns,
        out_shape=(pltpu.VMEM(weight.shape, weight.dtype), pltpu.VMEM(out_weight.shape, out_weight.dtype))
        + (jax.ShapeDtypeStruct((width, width), out_weight.dtype),) * columns,
        scratch_shapes=[pltpu.SemaphoreType.DMA((columns + 2,))],
        compiler_params=pltpu.CompilerParams(vmem_limit_bytes=VMEM_LIMIT),
        cost_estimate=pl.CostEstimate(flops=0, bytes_accessed=weight.size // 8, transcendentals=0),
    )(ids, weight, out_weight)


def project_body(step, ids_ref, mine_ref, theirs_ref, weight_ref, other_ref, out_ref):
    width = other_ref.shape[0]
    at = pl.ds(pl.multiple_of(lax.bitwise_xor(ids_ref[0], step) * width, HD), width)
    total = jnp.dot(mine_ref[...], weight_ref[:, at], preferred_element_type=F32)
    total = total + jnp.dot(theirs_ref[...], other_ref[...], preferred_element_type=F32)
    out_ref[...] = total.astype(out_ref.dtype)


def project(ids, mine, theirs, weight, other, step, dtype):
    rows, width = mine.shape
    vmem = pl.BlockSpec(memory_space=pltpu.VMEM)
    pin = lambda x: pltpu.with_memory_space_constraint(x, pltpu.VMEM)
    return pl.pallas_call(
        functools.partial(project_body, step),
        in_specs=[pl.BlockSpec(memory_space=pltpu.SMEM)] + [vmem] * 4,
        out_specs=vmem,
        out_shape=jax.ShapeDtypeStruct((rows, width), dtype),
        compiler_params=pltpu.CompilerParams(vmem_limit_bytes=VMEM_LIMIT),
        cost_estimate=pl.CostEstimate(
            flops=rows * width * width * (4 if step else 64), bytes_accessed=rows * width, transcendentals=0
        ),
    )(ids, mine, theirs, pin(weight), pin(other))


def cross(piece):
    size = lax.axis_size("ha")
    return [piece] + [flip(piece, "ha", step) for step in range(2, size, 2)]


def paired(pieces):
    return [shard for piece in pieces for shard in (piece, flip(piece, "ha", 1))]


def spread(piece):
    return paired(cross(piece))


def after_all(pieces, other):
    return [pieces[0]] + [after(piece, other) for piece in pieces[1:]]


def after(x, *others):
    return lax.optimization_barrier((x, *others))[0]


def on_device(latents, timesteps, mod_weight, qkv_weight, out_weight, noise_frame):
    frames, tok_count, width = latents.shape
    ha_size, pb_size = lax.axis_size("ha"), lax.axis_size("pb")
    ha, pb = lax.axis_index("ha"), lax.axis_index("pb")
    ids = jnp.stack([ha, pb]).astype(jnp.int32)
    piece = latents.reshape(tok_count, width)
    weight = jnp.transpose(qkv_weight, (1, 0, 2))

    embedding = sinusoid(timesteps).astype(BF16)
    modulation = jnp.einsum(
        "pe,jef->pjf", embedding, jnp.transpose(mod_weight, (1, 0, 2)), preferred_element_type=F32
    ).astype(BF16)
    gate = modulation[:, 2].astype(F32)
    mod_rows = jnp.pad(modulation[0, :2], ((0, MOD_ROWS - 2), (0, 0)))
    carried = jnp.concatenate([mod_rows, piece], axis=0)

    weight, out_local, *columns = fetch(after(ids, carried), weight, out_weight, ha_size)
    other_weight = [flip(c, "ha", 1) for c in columns]

    def frame(pieces, state, mods=None, last=False):
        got = frame_step(ids, pieces, mods, weight, state, last, 0 if mods else MOD_ROWS)
        return got[0] if last else got if state is None else (state[0], *got)

    half = MOD_ROWS + tok_count // 2
    if pb_size == 4:
        pairs, middle, outward = [(0, 1), (1, 0), (2, 3), (3, 2)], [(1, 2), (2, 1)], [(1, 0), (2, 3)]
        first = after(lax.ppermute(carried, "pb", pairs), weight)
        crossed = after(lax.ppermute(carried, "pb", middle), weight)
        own = cross(carried)
        first_over = cross(first)
        beyond = lax.ppermute(crossed, "pb", outward)
        passed = lax.ppermute(first, "pb", middle)
        state = frame(paired(after_all(own, weight)), None)
        beyond, passed = after(beyond, state[0]), after(passed, state[0])
        second = crossed + beyond
        second_over = cross(second)
        onward = lax.ppermute(passed, "pb", outward)
        state = frame(paired([after(p, state[0]) for p in first_over]), state)
        third = passed + after(onward, state[1])
        third_parts = [cross(third[:half]), cross(third[half:])]
        state = frame(paired([after(p, state[1]) for p in second_over]), state)
        pieces = paired([after(p, state[1]) for p in third_parts[0]])
        state = frame(pieces, state)
        attended = frame(paired([after(p, state[1]) for p in third_parts[1]]), state, pieces, True)
    else:
        state = frame(spread(carried), None)
        for bit in range(1, pb_size):
            state = frame(spread(flip(carried, "pb", bit)), state, None, bit == pb_size - 1)
        attended = state

    is_last = pb == pb_size - 1
    done, following = [], []
    chunk = tok_count // 3
    parts = []
    for start in range(0, tok_count, chunk):
        mine = attended[start : start + chunk]
        both = (mine, flip(mine, "ha", 1))
        sent = [
            flip(project(ids, *both, out_local, other_weight[step // 2], step, BF16), "ha", step)
            for step in range(2, ha_size, 2)
        ]
        parts.append((start, both, sent))
    for start, both, sent in parts:
        both = tuple(after(x, *done[-1:]) for x in both)
        branch = project(ids, *both, out_local, other_weight[0], 0, F32)
        for part in sent:
            part = after(part, *done[-1:])
            branch = branch + part.astype(F32)
        advanced = (piece[start : start + chunk].astype(F32) + gate * branch).astype(BF16)
        done.append(advanced)
        following.append(from_behind(advanced, "pb", -1))
    following = [
        jnp.where(is_last, noise_frame[n * chunk : (n + 1) * chunk], incoming) for n, incoming in enumerate(following)
    ]
    return jnp.concatenate(done, axis=0)[None], jnp.concatenate(following, axis=0)[None]


def solution(mesh):
    placed = (
        P(("grp", "pb"), None, "ha"),
        P(("grp", "pb")),
        P(None, None, "ha"),
        P(None, None, "ha"),
        P("ha", None),
        P("grp", "ha"),
    )
    return jax.shard_map(
        on_device,
        mesh=mesh,
        in_specs=placed,
        out_specs=(P(("grp", "pb"), None, "ha"), P(("grp", "pb"), None, "ha")),
        check_vma=False,
    )
```

```python
import functools
import math

import jax
import jax.numpy as jnp
from jax import lax
from jax.experimental import pallas as pl
from jax.experimental.pallas import tpu as pltpu
from jax.sharding import PartitionSpec as P

HD = 128
TDIM = 256
F32 = jnp.float32
BF16 = jnp.bfloat16
VMEM_LIMIT = 20 * 1024 * 1024
MOD_ROWS = 16


def flip(x, axis, bit):
    size = lax.axis_size(axis)
    return lax.ppermute(x, axis, [(i, i ^ bit) for i in range(size)])


def from_behind(x, axis, by):
    size = lax.axis_size(axis)
    pairs = [(i, i + by) for i in range(size) if 0 <= i + by < size]
    return lax.ppermute(x, axis, pairs)


def sinusoid(timesteps):
    half_width = TDIM // 2
    frequency = jnp.exp(-math.log(10000.0) * jnp.arange(half_width, dtype=F32) / half_width)
    angles = timesteps.astype(F32)[:, None] * frequency[None, :]
    return jnp.concatenate([jnp.cos(angles), jnp.sin(angles)], axis=1)


def unit_rms(vectors):
    return vectors * lax.rsqrt(jnp.mean(vectors * vectors, axis=-1, keepdims=True) + 1e-06)


def norm_rows(ha, piece_refs, mod_refs, offset, hidden_ref, scale_ref, shift_ref):
    count = len(piece_refs)
    rows, full = hidden_ref.shape
    width = full // count
    step = 64
    spots = []
    for j in range(count):
        spot = pl.ds(pl.multiple_of(lax.bitwise_xor(ha, j) * width, HD), width)
        mod = mod_refs[j][0:MOD_ROWS, :].astype(F32)
        shift_ref[j] = jnp.broadcast_to(mod[0:1], (8, width))
        scale_ref[j] = jnp.broadcast_to(1.0 + mod[1:2], (8, width))
        spots.append(spot)

    def one(i, carry):
        at = pl.ds(pl.multiple_of(offset + i * step, 16), step)
        to = pl.ds(pl.multiple_of(i * step, step), step)

        def sum_rows(parts):
            total = None
            for part in parts:
                for k in range(0, width, HD):
                    tile = part[:, k : k + HD]
                    total = tile if total is None else total + tile
            return jnp.sum(total, axis=-1, keepdims=True) * (1.0 / full)

        mean = sum_rows(ref[at, :].astype(F32) for ref in piece_refs)
        inverse = lax.rsqrt(sum_rows(jnp.square(ref[at, :].astype(F32) - mean) for ref in piece_refs) + 1e-06)
        for j, ref in enumerate(piece_refs):
            normed = ((ref[at, :].astype(F32) - mean) * inverse).reshape(step // 8, 8, width)
            out = normed * scale_ref[j][None] + shift_ref[j][None]
            hidden_ref[to, spots[j]] = out.reshape(step, width).astype(BF16)
        return carry

    lax.fori_loop(0, rows // step, one, 0)


def attend(q, k, v, num, den):
    scores = lax.dot_general(q, k, (((1,), (1,)), ((), ())), preferred_element_type=F32)
    weights = jnp.exp(scores)
    for start in range(0, weights.shape[1], HD):
        part = weights[:, start : start + HD]
        if part.shape[1] < HD:
            part = jnp.concatenate([part, jnp.zeros((part.shape[0], HD - part.shape[1]), F32)], axis=1)
        den = part if den is None else den + part
    more = jnp.dot(weights.astype(BF16), v, preferred_element_type=F32)
    return more if num is None else num + more, den


def frame_body(own, last, count, offset, separate, ids_ref, *refs):
    refs = list(refs)
    pieces, refs = refs[:count], refs[count:]
    mods = pieces
    if separate:
        mods, refs = refs[:count], refs[count:]
    weight_ref, refs = refs[0], refs[1:]
    hidden_ref, scale_ref, shift_ref = refs[-3:]
    if own:
        q_out, num_out, den_out = refs[:-3]
    elif last:
        q_ref, num_ref, den_ref, att_out = refs[:-3]
    else:
        q_ref, num_ref, den_ref, num_out, den_out = refs[:-3]
    norm_rows(ids_ref[0], pieces, mods, offset, hidden_ref, scale_ref, shift_ref)
    width = weight_ref.shape[2]
    block = 2 * HD if width % (2 * HD) == 0 else HD
    for start in range(0, width, block):
        hidden = hidden_ref[...]
        columns = slice(start, start + block)
        key_all = jnp.dot(hidden, weight_ref[1, :, columns], preferred_element_type=F32)
        value_all = jnp.dot(hidden, weight_ref[2, :, columns], preferred_element_type=F32)
        query_all = jnp.dot(hidden, weight_ref[0, :, columns], preferred_element_type=F32) if own else None
        for head in range(0, block, HD):
            inner = slice(head, head + HD)
            at = slice(start + head, start + head + HD)
            k = unit_rms(key_all[:, inner]).astype(BF16)
            v = value_all[:, inner].astype(BF16)
            if own:
                q = (unit_rms(query_all[:, inner]) * (1.0 / math.sqrt(HD))).astype(BF16)
                q_out[:, at] = q
                num, den = attend(q, k, v, None, None)
            else:
                num, den = attend(q_ref[:, at], k, v, num_ref[:, at], den_ref[:, at])
            if last:
                att_out[:, at] = (num / jnp.sum(den, axis=-1, keepdims=True)).astype(BF16)
            else:
                num_out[:, at] = num
                den_out[:, at] = den


def frame_step(ids, pieces, mods, weight, state, last=False, offset=0):
    own = state is None
    count = len(pieces)
    width = pieces[0].shape[1]
    rows = pieces[0].shape[0] - offset
    full = weight.shape[1]
    queries = rows if own else state[0].shape[0]
    args = [*pieces, *(mods or ()), weight, *(state or ())]
    wide = jax.ShapeDtypeStruct((queries, width), F32)
    thin = jax.ShapeDtypeStruct((queries, width), BF16)
    outs = (thin, wide, wide) if own else (thin,) if last else (wide, wide)
    used = 3 if own else 2
    args = [pltpu.with_memory_space_constraint(x, pltpu.VMEM) if x is weight else x for x in args]
    vmem = pl.BlockSpec(memory_space=pltpu.VMEM)
    return pl.pallas_call(
        functools.partial(frame_body, own, last, count, offset, mods is not None),
        in_specs=[pl.BlockSpec(memory_space=pltpu.SMEM)] + [vmem] * len(args),
        out_specs=tuple(vmem for _ in outs),
        scratch_shapes=[
            pltpu.VMEM((rows, full), BF16),
            pltpu.VMEM((count, 8, width), F32),
            pltpu.VMEM((count, 8, width), F32),
        ],
        out_shape=outs,
        compiler_params=pltpu.CompilerParams(vmem_limit_bytes=VMEM_LIMIT),
        cost_estimate=pl.CostEstimate(
            flops=rows * full * width // 8, bytes_accessed=rows * full // 8, transcendentals=0
        ),
    )(ids, *args)


def fetch_body(ids_ref, weight_ref, out_ref, weight_out, out_out, columns_out, sems):
    width = out_ref.shape[0]
    copies = [
        pltpu.make_async_copy(weight_ref, weight_out, sems.at[0]),
        pltpu.make_async_copy(out_ref, out_out, sems.at[1]),
    ]
    for n in range(columns_out.shape[0]):
        at = pl.ds(pl.multiple_of(lax.bitwise_xor(ids_ref[0], 2 * n + 1) * width, HD), width)
        copies.append(pltpu.make_async_copy(out_ref.at[:, at], columns_out.at[n], sems.at[n + 2]))
    for copy in copies:
        copy.start()
    for copy in copies:
        copy.wait()


def fetch(ids, weight, out_weight, ha_size):
    width = out_weight.shape[0]
    columns = ha_size // 2
    anywhere, vmem = pl.BlockSpec(memory_space=pltpu.HBM), pl.BlockSpec(memory_space=pltpu.VMEM)
    return pl.pallas_call(
        fetch_body,
        in_specs=[pl.BlockSpec(memory_space=pltpu.SMEM), anywhere, anywhere],
        out_specs=(vmem, vmem, anywhere),
        out_shape=(pltpu.VMEM(weight.shape, weight.dtype), pltpu.VMEM(out_weight.shape, out_weight.dtype))
        + (jax.ShapeDtypeStruct((columns, width, width), out_weight.dtype),),
        scratch_shapes=[pltpu.SemaphoreType.DMA((columns + 2,))],
        compiler_params=pltpu.CompilerParams(vmem_limit_bytes=VMEM_LIMIT),
        cost_estimate=pl.CostEstimate(flops=0, bytes_accessed=weight.size // 8, transcendentals=0),
    )(ids, weight, out_weight)


def project_body(step, cuts, ids_ref, mine_ref, theirs_ref, weight_ref, other_ref, *out_refs):
    width = other_ref.shape[1]
    at = pl.ds(pl.multiple_of(lax.bitwise_xor(ids_ref[0], step) * width, HD), width)
    total = jnp.dot(mine_ref[...], weight_ref[:, at], preferred_element_type=F32)
    total = total + jnp.dot(theirs_ref[...], other_ref[step // 2], preferred_element_type=F32)
    for start, stop, out_ref in zip(cuts, cuts[1:], out_refs):
        out_ref[...] = total[start:stop].astype(out_ref.dtype)


def project(ids, mine, theirs, weight, other, step, cuts, dtype):
    rows, width = mine.shape
    vmem = pl.BlockSpec(memory_space=pltpu.VMEM)
    pin = lambda x: pltpu.with_memory_space_constraint(x, pltpu.VMEM)
    outs = tuple(jax.ShapeDtypeStruct((stop - start, width), dtype) for start, stop in zip(cuts, cuts[1:]))
    return pl.pallas_call(
        functools.partial(project_body, step, cuts),
        in_specs=[pl.BlockSpec(memory_space=pltpu.SMEM)] + [vmem] * 4,
        out_specs=(vmem,) * len(outs),
        out_shape=outs,
        compiler_params=pltpu.CompilerParams(vmem_limit_bytes=VMEM_LIMIT),
        cost_estimate=pl.CostEstimate(
            flops=rows * width * width // 4, bytes_accessed=rows * width // 4, transcendentals=0
        ),
    )(ids, mine, theirs, pin(weight), pin(other))


def cross(piece):
    size = lax.axis_size("ha")
    return [piece] + [flip(piece, "ha", step) for step in range(2, size, 2)]


def paired(pieces):
    return [shard for piece in pieces for shard in (piece, flip(piece, "ha", 1))]


def spread(piece):
    return paired(cross(piece))


def after_all(pieces, other):
    return [pieces[0]] + [after(piece, other) for piece in pieces[1:]]


def after(x, *others):
    return lax.optimization_barrier((x, *others))[0]


def on_device(latents, timesteps, mod_weight, qkv_weight, out_weight, noise_frame):
    frames, tok_count, width = latents.shape
    ha_size, pb_size = lax.axis_size("ha"), lax.axis_size("pb")
    ha, pb = lax.axis_index("ha"), lax.axis_index("pb")
    ids = jnp.stack([ha, pb]).astype(jnp.int32)
    piece = latents.reshape(tok_count, width)
    weight = jnp.transpose(qkv_weight, (1, 0, 2))

    embedding = sinusoid(timesteps).astype(BF16)
    modulation = jnp.einsum(
        "pe,jef->pjf", embedding, jnp.transpose(mod_weight, (1, 0, 2)), preferred_element_type=F32
    ).astype(BF16)
    gate = modulation[:, 2].astype(F32)
    mod_rows = jnp.pad(modulation[0, :2], ((0, MOD_ROWS - 2), (0, 0)))
    carried = jnp.concatenate([mod_rows, piece], axis=0)

    weight, out_local, columns = fetch(after(ids, carried), weight, out_weight, ha_size)

    def frame(pieces, state, mods=None, last=False):
        got = frame_step(ids, pieces, mods, weight, state, last, 0 if mods else MOD_ROWS)
        return got[0] if last else got if state is None else (state[0], *got)

    if pb_size == 4:
        pairs, middle, outward = [(0, 1), (1, 0), (2, 3), (3, 2)], [(1, 2), (2, 1)], [(1, 0), (2, 3)]
        own = cross(carried)
        first = after(lax.ppermute(carried, "pb", pairs), weight)
        first_over = cross(first)
        passed = lax.ppermute(first, "pb", middle)
        crossed = after(lax.ppermute(carried, "pb", middle), weight, first)
        beyond = lax.ppermute(crossed, "pb", outward)
        state = frame(paired(after_all(own, weight)), None)
        passed = after(passed, state[0])
        onward = lax.ppermute(passed, "pb", outward)
        second = crossed + after(beyond, passed)
        second_over = cross(second)
        state = frame(paired([after(p, passed) for p in first_over]), state)
        third = cross(passed + after(onward, state[1]))
        state = frame(paired([after(p, state[1]) for p in second_over]), state)
        rest = paired([after(p, state[1]) for p in third])
        other_weight = flip(after(columns, *rest), "ha", 1)
        attended = frame(rest, state, None, True)
    else:
        other_weight = flip(columns, "ha", 1)
        state = frame(spread(carried), None)
        for bit in range(1, pb_size):
            state = frame(spread(flip(carried, "pb", bit)), state, None, bit == pb_size - 1)
        attended = state

    is_last = pb == pb_size - 1
    done, following = [], []
    cuts = (0, tok_count // 3, 2 * tok_count // 3, tok_count)
    both = (attended, flip(attended, "ha", 1))
    sent = []
    for step in range(2, ha_size, 2):
        parts = project(ids, *both, out_local, other_weight, step, cuts, BF16)
        sent.append([flip(part, "ha", step) for part in parts])
    mine = project(ids, *both, out_local, other_weight, 0, cuts, F32)
    for n, (start, stop, branch) in enumerate(zip(cuts, cuts[1:], mine)):
        for parts in sent:
            part = after(parts[n], *mine, *done[-1:])
            branch = branch + part.astype(F32)
        advanced = (piece[start:stop].astype(F32) + gate * branch).astype(BF16)
        done.append(advanced)
        following.append(from_behind(advanced, "pb", -1))
    following = [after(part, *following[:n]) for n, part in enumerate(following)]
    queue_next = jnp.where(is_last, noise_frame, jnp.concatenate(following, axis=0))
    return jnp.concatenate(done, axis=0)[None], queue_next[None]


def solution(mesh):
    placed = (
        P(("grp", "pb"), None, "ha"),
        P(("grp", "pb")),
        P(None, None, "ha"),
        P(None, None, "ha"),
        P("ha", None),
        P("grp", "ha"),
    )
    return jax.shard_map(
        on_device,
        mesh=mesh,
        in_specs=placed,
        out_specs=(P(("grp", "pb"), None, "ha"), P(("grp", "pb"), None, "ha")),
        check_vma=False,
    )
```

```python
import functools
import math

import jax
import jax.numpy as jnp
from jax import lax
from jax.experimental import pallas as pl
from jax.experimental.pallas import tpu as pltpu
from jax.sharding import PartitionSpec as P

HD = 128
TDIM = 256
F32 = jnp.float32
BF16 = jnp.bfloat16
VMEM_LIMIT = 20 * 1024 * 1024
MOD_ROWS = 16
PARTS = 2


def flip(x, axis, bit):
    size = lax.axis_size(axis)
    return lax.ppermute(x, axis, [(i, i ^ bit) for i in range(size)])


def from_behind(x, axis, by):
    size = lax.axis_size(axis)
    pairs = [(i, i + by) for i in range(size) if 0 <= i + by < size]
    return lax.ppermute(x, axis, pairs)


def sinusoid(timesteps):
    half_width = TDIM // 2
    frequency = jnp.exp(-math.log(10000.0) * jnp.arange(half_width, dtype=F32) / half_width)
    angles = timesteps.astype(F32)[:, None] * frequency[None, :]
    return jnp.concatenate([jnp.cos(angles), jnp.sin(angles)], axis=1)


def unit_rms(vectors):
    return vectors * lax.rsqrt(jnp.mean(vectors * vectors, axis=-1, keepdims=True) + 1e-06)


def norm_rows(ha, pieces, hidden_ref, scale_ref, shift_ref):
    count = len(pieces)
    rows, full = hidden_ref.shape
    width = full // count
    step = 64
    spots = []
    for j, parts in enumerate(pieces):
        spot = pl.ds(pl.multiple_of(lax.bitwise_xor(ha, j) * width, HD), width)
        mod = parts[0][0:MOD_ROWS, :].astype(F32)
        shift_ref[j] = jnp.broadcast_to(mod[0:1], (8, width))
        scale_ref[j] = jnp.broadcast_to(1.0 + mod[1:2], (8, width))
        spots.append(spot)

    def sum_rows(tiles):
        total = None
        for tile in tiles:
            for k in range(0, width, HD):
                part = tile[:, k : k + HD]
                total = part if total is None else total + part
        return jnp.sum(total, axis=-1, keepdims=True) * (1.0 / full)

    def some_rows(sources, target, size):
        def one(i, carry):
            to = pl.ds(pl.multiple_of(target + i * step, step), step)
            spans = [(ref, pl.ds(pl.multiple_of(offset + i * step, 16), step)) for ref, offset in sources]
            mean = sum_rows(ref[at, :].astype(F32) for ref, at in spans)
            inverse = lax.rsqrt(sum_rows(jnp.square(ref[at, :].astype(F32) - mean) for ref, at in spans) + 1e-06)
            for j, (ref, at) in enumerate(spans):
                normed = ((ref[at, :].astype(F32) - mean) * inverse).reshape(step // 8, 8, width)
                out = normed * scale_ref[j][None] + shift_ref[j][None]
                hidden_ref[to, spots[j]] = out.reshape(step, width).astype(BF16)
            return carry

        lax.fori_loop(0, size // step, one, 0)

    cuts = [0] + [MOD_ROWS + rows * n // PARTS for n in range(1, PARTS + 1)]
    for n in range(PARTS):
        skip = MOD_ROWS if n == 0 else 0
        sources = [(parts[n], skip) if len(parts) > 1 else (parts[0], cuts[n] + skip) for parts in pieces]
        some_rows(sources, cuts[n] + skip - MOD_ROWS, cuts[n + 1] - cuts[n] - skip)


def attend(q, k, v, num, den):
    scores = lax.dot_general(q, k, (((1,), (1,)), ((), ())), preferred_element_type=F32)
    weights = jnp.exp(scores)
    for start in range(0, weights.shape[1], HD):
        part = weights[:, start : start + HD]
        if part.shape[1] < HD:
            part = jnp.concatenate([part, jnp.zeros((part.shape[0], HD - part.shape[1]), F32)], axis=1)
        den = part if den is None else den + part
    more = jnp.dot(weights.astype(BF16), v, preferred_element_type=F32)
    return more if num is None else num + more, den


def frame_body(own, fresh, last, splits, ids_ref, *refs):
    refs = list(refs)
    pieces = []
    for split in splits:
        pieces.append(refs[:split])
        refs = refs[split:]
    weight_ref, refs = refs[0], refs[1:]
    hidden_ref, scale_ref, shift_ref = refs[-3:]
    if own:
        q_out, k_out, v_out = refs[:-3]
    else:
        q_ref, *refs = refs[:-3]
        if not fresh:
            num_ref, den_ref, *refs = refs
        if last:
            (att_out,) = refs
        else:
            num_out, den_out = refs
    norm_rows(ids_ref[0], pieces, hidden_ref, scale_ref, shift_ref)
    width = weight_ref.shape[2]
    block = 2 * HD if width % (2 * HD) == 0 else HD
    for start in range(0, width, block):
        hidden = hidden_ref[...]
        columns = slice(start, start + block)
        key_all = jnp.dot(hidden, weight_ref[1, :, columns], preferred_element_type=F32)
        value_all = jnp.dot(hidden, weight_ref[2, :, columns], preferred_element_type=F32)
        query_all = jnp.dot(hidden, weight_ref[0, :, columns], preferred_element_type=F32) if own else None
        for head in range(0, block, HD):
            inner = slice(head, head + HD)
            at = slice(start + head, start + head + HD)
            k = unit_rms(key_all[:, inner]).astype(BF16)
            v = value_all[:, inner].astype(BF16)
            if own:
                q_out[:, at] = (unit_rms(query_all[:, inner]) * (1.0 / math.sqrt(HD))).astype(BF16)
                k_out[:, at] = k
                v_out[:, at] = v
                continue
            before = (None, None) if fresh else (num_ref[:, at], den_ref[:, at])
            num, den = attend(q_ref[:, at], k, v, *before)
            if last:
                att_out[:, at] = (num / jnp.sum(den, axis=-1, keepdims=True)).astype(BF16)
            else:
                num_out[:, at] = num
                den_out[:, at] = den


def frame_step(ids, pieces, weight, state, last=False):
    own = state is None
    pieces = [piece if isinstance(piece, tuple) else (piece,) for piece in pieces]
    count = len(pieces)
    width = pieces[0][0].shape[1]
    rows = sum(part.shape[0] for part in pieces[0]) - MOD_ROWS
    full = weight.shape[1]
    queries = rows if own else state[0].shape[0]
    args = [*(part for piece in pieces for part in piece), weight, *(state or ())]
    wide = jax.ShapeDtypeStruct((queries, width), F32)
    thin = jax.ShapeDtypeStruct((queries, width), BF16)
    outs = (thin, thin, thin) if own else (thin,) if last else (wide, wide)
    fresh = not own and len(state) == 1
    used = 3 if own else 2
    args = [pltpu.with_memory_space_constraint(x, pltpu.VMEM) if x is weight else x for x in args]
    vmem = pl.BlockSpec(memory_space=pltpu.VMEM)
    return pl.pallas_call(
        functools.partial(frame_body, own, fresh, last, [len(piece) for piece in pieces]),
        in_specs=[pl.BlockSpec(memory_space=pltpu.SMEM)] + [vmem] * len(args),
        out_specs=tuple(vmem for _ in outs),
        scratch_shapes=[
            pltpu.VMEM((rows, full), BF16),
            pltpu.VMEM((count, 8, width), F32),
            pltpu.VMEM((count, 8, width), F32),
        ],
        out_shape=outs,
        compiler_params=pltpu.CompilerParams(vmem_limit_bytes=VMEM_LIMIT),
        cost_estimate=pl.CostEstimate(
            flops=rows * full * width // 8, bytes_accessed=rows * full // 8, transcendentals=0
        ),
    )(ids, *args)


def own_body(q_ref, k_ref, v_ref, num_ref, den_ref, num_out, den_out):
    for start in range(0, q_ref.shape[1], HD):
        at = slice(start, start + HD)
        num_out[:, at], den_out[:, at] = attend(q_ref[:, at], k_ref[:, at], v_ref[:, at], num_ref[:, at], den_ref[:, at])


def own_step(q, k, v, num, den):
    vmem = pl.BlockSpec(memory_space=pltpu.VMEM)
    wide = jax.ShapeDtypeStruct(num.shape, F32)
    return pl.pallas_call(
        own_body,
        in_specs=[vmem] * 5,
        out_specs=(vmem, vmem),
        out_shape=(wide, wide),
        compiler_params=pltpu.CompilerParams(vmem_limit_bytes=VMEM_LIMIT),
        cost_estimate=pl.CostEstimate(flops=q.size, bytes_accessed=q.size, transcendentals=0),
    )(q, k, v, num, den)


def place_body(last_ref, incoming_ref, noise_ref, *refs):
    refs[-1][...] = jnp.where(last_ref[0] != 0, noise_ref[...], incoming_ref[...])


def place(n, is_last, incoming, noise_frame, queue):
    block = pl.BlockSpec(incoming.shape, lambda i: (n, 0))
    whole = pl.BlockSpec(incoming.shape, lambda i: (0, 0))
    before = [] if queue is None else [queue]
    return pl.pallas_call(
        place_body,
        grid=(1,),
        in_specs=[pl.BlockSpec(memory_space=pltpu.SMEM), whole, block] + [pl.BlockSpec(memory_space=pl.ANY)] * len(before),
        out_specs=block,
        out_shape=jax.ShapeDtypeStruct(noise_frame.shape, noise_frame.dtype),
        input_output_aliases={3: 0} if before else {},
        compiler_params=pltpu.CompilerParams(vmem_limit_bytes=VMEM_LIMIT),
        cost_estimate=pl.CostEstimate(flops=10**9, bytes_accessed=incoming.size, transcendentals=0),
    )(is_last, incoming, noise_frame, *before)


def add_body(a_ref, b_ref, out_ref):
    out_ref[...] = a_ref[...] + b_ref[...]


def add(a, b):
    vmem = pl.BlockSpec(memory_space=pltpu.VMEM)
    return pl.pallas_call(
        add_body,
        in_specs=[vmem, vmem],
        out_specs=vmem,
        out_shape=jax.ShapeDtypeStruct(a.shape, a.dtype),
        compiler_params=pltpu.CompilerParams(vmem_limit_bytes=VMEM_LIMIT),
        cost_estimate=pl.CostEstimate(flops=a.size // 8, bytes_accessed=a.size // 8, transcendentals=0),
    )(a, b)


def fetch_body(ids_ref, weight_ref, out_ref, weight_out, kept_out, sent_out, sems):
    width = out_ref.shape[0]
    copies = [pltpu.make_async_copy(weight_ref, weight_out, sems.at[0])]
    for n in range(kept_out.shape[0]):
        for core, target in enumerate((kept_out, sent_out)):
            at = pl.ds(pl.multiple_of(lax.bitwise_xor(ids_ref[0], 2 * n + core) * width, HD), width)
            copies.append(pltpu.make_async_copy(out_ref.at[:, at], target.at[n], sems.at[len(copies)]))
    for copy in copies:
        copy.start()
    for copy in copies:
        copy.wait()


def fetch(ids, weight, out_weight, ha_size):
    width = out_weight.shape[0]
    columns = ha_size // 2
    anywhere, vmem = pl.BlockSpec(memory_space=pl.ANY), pl.BlockSpec(memory_space=pltpu.VMEM)
    kept = pltpu.HBM((columns, width, width), out_weight.dtype)
    return pl.pallas_call(
        fetch_body,
        in_specs=[pl.BlockSpec(memory_space=pltpu.SMEM), anywhere, anywhere],
        out_specs=(vmem, anywhere, anywhere),
        out_shape=(pltpu.VMEM(weight.shape, weight.dtype), kept, kept),
        scratch_shapes=[pltpu.SemaphoreType.DMA((2 * columns + 1,))],
        compiler_params=pltpu.CompilerParams(vmem_limit_bytes=VMEM_LIMIT),
        cost_estimate=pl.CostEstimate(flops=0, bytes_accessed=weight.size // 8, transcendentals=0),
    )(ids, pltpu.with_memory_space_constraint(weight, pltpu.HBM), out_weight)


def project_body(step, cuts, mine_ref, theirs_ref, weight_ref, other_ref, *out_refs):
    first, end = cuts[0], cuts[-1]
    total = jnp.dot(mine_ref[first:end, :], weight_ref[step // 2], preferred_element_type=F32)
    total = total + jnp.dot(theirs_ref[first:end, :], other_ref[step // 2], preferred_element_type=F32)
    for start, stop, out_ref in zip(cuts, cuts[1:], out_refs):
        out_ref[...] = total[start - first : stop - first].astype(out_ref.dtype)


def project(mine, theirs, weight, other, step, cuts, dtype):
    width = mine.shape[1]
    rows = cuts[-1] - cuts[0]
    vmem = pl.BlockSpec(memory_space=pltpu.VMEM)
    pin = lambda x: pltpu.with_memory_space_constraint(x, pltpu.VMEM)
    outs = tuple(jax.ShapeDtypeStruct((stop - start, width), dtype) for start, stop in zip(cuts, cuts[1:]))
    return pl.pallas_call(
        functools.partial(project_body, step, cuts),
        in_specs=[vmem] * 4,
        out_specs=(vmem,) * len(outs),
        out_shape=outs,
        compiler_params=pltpu.CompilerParams(vmem_limit_bytes=VMEM_LIMIT),
        cost_estimate=pl.CostEstimate(
            flops=rows * width * width // 4, bytes_accessed=rows * width // 4, transcendentals=0
        ),
    )(mine, theirs, pin(weight), pin(other))


def cross(piece):
    size = lax.axis_size("ha")
    return [piece] + [flip(piece, "ha", step) for step in range(2, size, 2)]


def swap(piece):
    rows = piece.shape[0] - MOD_ROWS
    cuts = [0] + [MOD_ROWS + rows * n // PARTS for n in range(1, PARTS + 1)]
    return tuple(flip(piece[start:stop], "ha", 1) for start, stop in zip(cuts, cuts[1:]))


def paired(pieces):
    return [shard for piece in pieces for shard in (piece, swap(piece))]


def spread(piece):
    return paired(cross(piece))


def after_all(pieces, other):
    return [pieces[0]] + [after(piece, other) for piece in pieces[1:]]


def after(x, *others):
    return lax.optimization_barrier((x, *others))[0]


def on_device(latents, timesteps, mod_weight, qkv_weight, out_weight, noise_frame):
    frames, tok_count, width = latents.shape
    ha_size, pb_size = lax.axis_size("ha"), lax.axis_size("pb")
    ha, pb = lax.axis_index("ha"), lax.axis_index("pb")
    ids = jnp.stack([ha, pb]).astype(jnp.int32)
    piece = latents.reshape(tok_count, width)
    weight = jnp.transpose(qkv_weight, (1, 0, 2))

    embedding = sinusoid(timesteps).astype(BF16)
    modulation = jnp.einsum(
        "pe,jef->pjf", embedding, jnp.transpose(mod_weight, (1, 0, 2)), preferred_element_type=F32
    ).astype(BF16)
    gate = modulation[:, 2].astype(F32)
    mod_rows = jnp.pad(modulation[0, :2], ((0, MOD_ROWS - 2), (0, 0)))
    carried = jnp.concatenate([mod_rows, piece], axis=0)

    weight, out_local, columns = fetch(after(ids, carried), weight, out_weight, ha_size)

    def frame(pieces, state=None, last=False):
        got = frame_step(ids, pieces, weight, state, last)
        return got[0] if last else got if state is None else (state[0], *got)

    if pb_size == 4:
        pairs, middle, outward = [(0, 1), (1, 0), (2, 3), (3, 2)], [(1, 2), (2, 1)], [(1, 0), (2, 3)]
        own = cross(carried)
        first = after(lax.ppermute(carried, "pb", pairs), weight)
        first_over = cross(first)
        passed = lax.ppermute(first, "pb", middle)
        crossed = after(lax.ppermute(carried, "pb", middle), weight, first)
        beyond = lax.ppermute(crossed, "pb", outward)
        q, k, v = frame(paired(after_all(own, weight)))
        passed = after(passed, q)
        onward = lax.ppermute(passed, "pb", outward)
        second = add(crossed, after(beyond, passed))
        second_over = cross(second)
        state = frame(paired([after(p, passed) for p in first_over]), (q,))
        third = cross(add(passed, after(onward, state[1])))
        state = (q, *own_step(q, k, v, *state[1:]))
        state = frame(paired([after(p, state[1]) for p in second_over]), state)
        rest = paired([after(p, state[1]) for p in third])
        other_weight = flip(after(columns, rest), "ha", 1)
        attended = frame(rest, state, True)
    else:
        other_weight = flip(columns, "ha", 1)
        q, k, v = frame(spread(carried))
        state = (q,)
        for bit in range(1, pb_size):
            state = frame(spread(flip(carried, "pb", bit)), state, bit == pb_size - 1)
            if bit == 1:
                state = (q, *own_step(q, k, v, *state[1:]))
        attended = state

    is_last = (pb == pb_size - 1).astype(jnp.int32).reshape(1)
    done, following = [], []
    cuts = tuple(tok_count * n // 3 for n in range(4))
    theirs = flip(attended, "ha", 1)
    sent = []
    for step in range(2, ha_size, 2):
        parts = []
        for at in zip(cuts, cuts[1:]):
            parts += project(after(attended, *parts[-1:]), theirs, out_local, other_weight, step, at, BF16)
        sent.append([flip(part, "ha", step) for part in parts])
    mine = project(attended, theirs, out_local, other_weight, 0, cuts, F32)
    for n, (start, stop, branch) in enumerate(zip(cuts, cuts[1:], mine)):
        for parts in sent:
            part = after(parts[n], *mine, *done[-1:])
            branch = branch + part.astype(F32)
        advanced = (piece[start:stop].astype(F32) + gate * branch).astype(BF16)
        done.append(advanced)
        following.append(from_behind(advanced, "pb", -1))
    queue = None
    for n, incoming in enumerate(following):
        queue = place(n, is_last, incoming if n == 0 else after(incoming, queue), noise_frame, queue)
    return jnp.concatenate(done, axis=0)[None], queue[None]


def solution(mesh):
    placed = (
        P(("grp", "pb"), None, "ha"),
        P(("grp", "pb")),
        P(None, None, "ha"),
        P(None, None, "ha"),
        P("ha", None),
        P("grp", "ha"),
    )
    return jax.shard_map(
        on_device,
        mesh=mesh,
        in_specs=placed,
        out_specs=(P(("grp", "pb"), None, "ha"), P(("grp", "pb"), None, "ha")),
        check_vma=False,
    )
```

```python
import functools
import math

import jax
import jax.numpy as jnp
from jax import lax
from jax.experimental import pallas as pl
from jax.experimental.pallas import tpu as pltpu
from jax.sharding import PartitionSpec as P

HD = 128
TDIM = 256
F32 = jnp.float32
BF16 = jnp.bfloat16
VMEM_LIMIT = 20 * 1024 * 1024
MOD_ROWS = 16
PARTS = 2


def flip(x, axis, bit):
    size = lax.axis_size(axis)
    return lax.ppermute(x, axis, [(i, i ^ bit) for i in range(size)])


def from_behind(x, axis, by):
    size = lax.axis_size(axis)
    pairs = [(i, i + by) for i in range(size) if 0 <= i + by < size]
    return lax.ppermute(x, axis, pairs)


def sinusoid(timesteps):
    half_width = TDIM // 2
    frequency = jnp.exp(-math.log(10000.0) * jnp.arange(half_width, dtype=F32) / half_width)
    angles = timesteps.astype(F32)[:, None] * frequency[None, :]
    return jnp.concatenate([jnp.cos(angles), jnp.sin(angles)], axis=1)


def unit_rms(vectors):
    return vectors * lax.rsqrt(jnp.mean(vectors * vectors, axis=-1, keepdims=True) + 1e-06)


def norm_rows(ha, pieces, hidden_ref, scale_ref, shift_ref):
    count = len(pieces)
    rows, full = hidden_ref.shape
    width = full // count
    step = 64
    spots = []
    for j, parts in enumerate(pieces):
        spot = pl.ds(pl.multiple_of(lax.bitwise_xor(ha, j) * width, HD), width)
        mod = parts[0][0:MOD_ROWS, :].astype(F32)
        shift_ref[j] = jnp.broadcast_to(mod[0:1], (8, width))
        scale_ref[j] = jnp.broadcast_to(1.0 + mod[1:2], (8, width))
        spots.append(spot)

    def sum_rows(tiles):
        total = None
        for tile in tiles:
            for k in range(0, width, HD):
                part = tile[:, k : k + HD]
                total = part if total is None else total + part
        return jnp.sum(total, axis=-1, keepdims=True) * (1.0 / full)

    def some_rows(sources, target, size):
        def one(i, carry):
            to = pl.ds(pl.multiple_of(target + i * step, step), step)
            spans = [(ref, pl.ds(pl.multiple_of(offset + i * step, 16), step)) for ref, offset in sources]
            mean = sum_rows(ref[at, :].astype(F32) for ref, at in spans)
            inverse = lax.rsqrt(sum_rows(jnp.square(ref[at, :].astype(F32) - mean) for ref, at in spans) + 1e-06)
            for j, (ref, at) in enumerate(spans):
                normed = ((ref[at, :].astype(F32) - mean) * inverse).reshape(step // 8, 8, width)
                out = normed * scale_ref[j][None] + shift_ref[j][None]
                hidden_ref[to, spots[j]] = out.reshape(step, width).astype(BF16)
            return carry

        lax.fori_loop(0, size // step, one, 0)

    cuts = [0] + [MOD_ROWS + rows * n // PARTS for n in range(1, PARTS + 1)]
    for n in range(PARTS):
        skip = MOD_ROWS if n == 0 else 0
        sources = [(parts[n], skip) if len(parts) > 1 else (parts[0], cuts[n] + skip) for parts in pieces]
        some_rows(sources, cuts[n] + skip - MOD_ROWS, cuts[n + 1] - cuts[n] - skip)


def attend(q, k, v, num, den):
    scores = lax.dot_general(q, k, (((1,), (1,)), ((), ())), preferred_element_type=F32)
    weights = jnp.exp(scores)
    for start in range(0, weights.shape[1], HD):
        part = weights[:, start : start + HD]
        if part.shape[1] < HD:
            part = jnp.concatenate([part, jnp.zeros((part.shape[0], HD - part.shape[1]), F32)], axis=1)
        den = part if den is None else den + part
    more = jnp.dot(weights.astype(BF16), v, preferred_element_type=F32)
    return more if num is None else num + more, den


def frame_body(own, fresh, last, splits, ids_ref, *refs):
    refs = list(refs)
    pieces = []
    for split in splits:
        pieces.append(refs[:split])
        refs = refs[split:]
    weight_ref, refs = refs[0], refs[1:]
    hidden_ref, scale_ref, shift_ref = refs[-3:]
    if own:
        q_out, k_out, v_out = refs[:-3]
    else:
        q_ref, *refs = refs[:-3]
        if not fresh:
            num_ref, den_ref, *refs = refs
        if last:
            (att_out,) = refs
        else:
            num_out, den_out = refs
    norm_rows(ids_ref[0], pieces, hidden_ref, scale_ref, shift_ref)
    width = weight_ref.shape[2]
    block = 2 * HD if width % (2 * HD) == 0 else HD
    for start in range(0, width, block):
        hidden = hidden_ref[...]
        columns = slice(start, start + block)
        key_all = jnp.dot(hidden, weight_ref[1, :, columns], preferred_element_type=F32)
        value_all = jnp.dot(hidden, weight_ref[2, :, columns], preferred_element_type=F32)
        query_all = jnp.dot(hidden, weight_ref[0, :, columns], preferred_element_type=F32) if own else None
        for head in range(0, block, HD):
            inner = slice(head, head + HD)
            at = slice(start + head, start + head + HD)
            k = unit_rms(key_all[:, inner]).astype(BF16)
            v = value_all[:, inner].astype(BF16)
            if own:
                q_out[:, at] = (unit_rms(query_all[:, inner]) * (1.0 / math.sqrt(HD))).astype(BF16)
                k_out[:, at] = k
                v_out[:, at] = v
                continue
            before = (None, None) if fresh else (num_ref[:, at], den_ref[:, at])
            num, den = attend(q_ref[:, at], k, v, *before)
            if last:
                att_out[:, at] = (num / jnp.sum(den, axis=-1, keepdims=True)).astype(BF16)
            else:
                num_out[:, at] = num
                den_out[:, at] = den


def frame_step(ids, pieces, weight, state, last=False):
    own = state is None
    pieces = [piece if isinstance(piece, tuple) else (piece,) for piece in pieces]
    count = len(pieces)
    width = pieces[0][0].shape[1]
    rows = sum(part.shape[0] for part in pieces[0]) - MOD_ROWS
    full = weight.shape[1]
    queries = rows if own else state[0].shape[0]
    args = [*(part for piece in pieces for part in piece), weight, *(state or ())]
    wide = jax.ShapeDtypeStruct((queries, width), F32)
    thin = jax.ShapeDtypeStruct((queries, width), BF16)
    outs = (thin, thin, thin) if own else (thin,) if last else (wide, wide)
    fresh = not own and len(state) == 1
    used = 3 if own else 2
    args = [pltpu.with_memory_space_constraint(x, pltpu.VMEM) if x is weight else x for x in args]
    vmem = pl.BlockSpec(memory_space=pltpu.VMEM)
    return pl.pallas_call(
        functools.partial(frame_body, own, fresh, last, [len(piece) for piece in pieces]),
        in_specs=[pl.BlockSpec(memory_space=pltpu.SMEM)] + [vmem] * len(args),
        out_specs=tuple(vmem for _ in outs),
        scratch_shapes=[
            pltpu.VMEM((rows, full), BF16),
            pltpu.VMEM((count, 8, width), F32),
            pltpu.VMEM((count, 8, width), F32),
        ],
        out_shape=outs,
        compiler_params=pltpu.CompilerParams(vmem_limit_bytes=VMEM_LIMIT),
        cost_estimate=pl.CostEstimate(
            flops=rows * full * width // 8, bytes_accessed=rows * full // 8, transcendentals=0
        ),
    )(ids, *args)


def own_body(q_ref, k_ref, v_ref, num_ref, den_ref, num_out, den_out):
    for start in range(0, q_ref.shape[1], HD):
        at = slice(start, start + HD)
        num_out[:, at], den_out[:, at] = attend(q_ref[:, at], k_ref[:, at], v_ref[:, at], num_ref[:, at], den_ref[:, at])


def own_step(q, k, v, num, den):
    vmem = pl.BlockSpec(memory_space=pltpu.VMEM)
    wide = jax.ShapeDtypeStruct(num.shape, F32)
    return pl.pallas_call(
        own_body,
        in_specs=[vmem] * 5,
        out_specs=(vmem, vmem),
        out_shape=(wide, wide),
        compiler_params=pltpu.CompilerParams(vmem_limit_bytes=VMEM_LIMIT),
        cost_estimate=pl.CostEstimate(flops=q.size, bytes_accessed=q.size, transcendentals=0),
    )(q, k, v, num, den)


def finish_body(latent_ref, gate_ref, *refs):
    *branch_refs, out_ref = refs
    branch = sum(ref[...].astype(F32) for ref in branch_refs)
    out_ref[...] = (latent_ref[...].astype(F32) + gate_ref[...] * branch).astype(BF16)


def finish(latents, gate, *branches):
    vmem = pl.BlockSpec(memory_space=pltpu.VMEM)
    return pl.pallas_call(
        finish_body,
        in_specs=[vmem] * (2 + len(branches)),
        out_specs=vmem,
        out_shape=jax.ShapeDtypeStruct(latents.shape, BF16),
        compiler_params=pltpu.CompilerParams(vmem_limit_bytes=VMEM_LIMIT),
        cost_estimate=pl.CostEstimate(flops=latents.size, bytes_accessed=latents.size, transcendentals=0),
    )(latents, gate, *branches)


def place_body(last_ref, incoming_ref, noise_ref, *refs):
    refs[-1][...] = jnp.where(last_ref[0] != 0, noise_ref[...], incoming_ref[...])


def place(n, is_last, incoming, noise_frame, queue):
    block = pl.BlockSpec((pl.Element(incoming.shape[0]), pl.Element(incoming.shape[1])), lambda i: (n, 0))
    whole = pl.BlockSpec(incoming.shape, lambda i: (0, 0))
    before = [] if queue is None else [queue]
    return pl.pallas_call(
        place_body,
        grid=(1,),
        in_specs=[pl.BlockSpec(memory_space=pltpu.SMEM), whole, block] + [pl.BlockSpec(memory_space=pl.ANY)] * len(before),
        out_specs=block,
        out_shape=jax.ShapeDtypeStruct(noise_frame.shape, noise_frame.dtype),
        input_output_aliases={3: 0} if before else {},
        compiler_params=pltpu.CompilerParams(vmem_limit_bytes=VMEM_LIMIT),
        cost_estimate=pl.CostEstimate(flops=10**9, bytes_accessed=incoming.size, transcendentals=0),
    )(is_last, incoming, noise_frame, *before)


def add_body(a_ref, b_ref, out_ref):
    out_ref[...] = a_ref[...] + b_ref[...]


def add(a, b):
    vmem = pl.BlockSpec(memory_space=pltpu.VMEM)
    return pl.pallas_call(
        add_body,
        in_specs=[vmem, vmem],
        out_specs=vmem,
        out_shape=jax.ShapeDtypeStruct(a.shape, a.dtype),
        compiler_params=pltpu.CompilerParams(vmem_limit_bytes=VMEM_LIMIT),
        cost_estimate=pl.CostEstimate(flops=a.size // 8, bytes_accessed=a.size // 8, transcendentals=0),
    )(a, b)


def fetch_body(ids_ref, weight_ref, out_ref, weight_out, kept_out, sent_out, sems):
    width = out_ref.shape[0]
    copies = [pltpu.make_async_copy(weight_ref, weight_out, sems.at[0])]
    for n in range(kept_out.shape[0]):
        for core, target in enumerate((kept_out, sent_out)):
            at = pl.ds(pl.multiple_of(lax.bitwise_xor(ids_ref[0], 2 * n + core) * width, HD), width)
            copies.append(pltpu.make_async_copy(out_ref.at[:, at], target.at[n], sems.at[len(copies)]))
    for copy in copies:
        copy.start()
    for copy in copies:
        copy.wait()


def fetch(ids, weight, out_weight, ha_size):
    width = out_weight.shape[0]
    columns = ha_size // 2
    anywhere, vmem = pl.BlockSpec(memory_space=pl.ANY), pl.BlockSpec(memory_space=pltpu.VMEM)
    kept = pltpu.HBM((columns, width, width), out_weight.dtype)
    return pl.pallas_call(
        fetch_body,
        in_specs=[pl.BlockSpec(memory_space=pltpu.SMEM), anywhere, anywhere],
        out_specs=(vmem, anywhere, anywhere),
        out_shape=(pltpu.VMEM(weight.shape, weight.dtype), kept, kept),
        scratch_shapes=[pltpu.SemaphoreType.DMA((2 * columns + 1,))],
        compiler_params=pltpu.CompilerParams(vmem_limit_bytes=VMEM_LIMIT),
        cost_estimate=pl.CostEstimate(flops=0, bytes_accessed=weight.size // 8, transcendentals=0),
    )(ids, pltpu.with_memory_space_constraint(weight, pltpu.HBM), out_weight)


def project_body(step, cuts, mine_ref, theirs_ref, weight_ref, other_ref, *out_refs):
    first, end = cuts[0], cuts[-1]
    total = jnp.dot(mine_ref[first:end, :], weight_ref[step // 2], preferred_element_type=F32)
    total = total + jnp.dot(theirs_ref[first:end, :], other_ref[step // 2], preferred_element_type=F32)
    for start, stop, out_ref in zip(cuts, cuts[1:], out_refs):
        out_ref[...] = total[start - first : stop - first].astype(out_ref.dtype)


def project(mine, theirs, weight, other, step, cuts, dtype):
    width = mine.shape[1]
    rows = cuts[-1] - cuts[0]
    vmem = pl.BlockSpec(memory_space=pltpu.VMEM)
    pin = lambda x: pltpu.with_memory_space_constraint(x, pltpu.VMEM)
    outs = tuple(jax.ShapeDtypeStruct((stop - start, width), dtype) for start, stop in zip(cuts, cuts[1:]))
    return pl.pallas_call(
        functools.partial(project_body, step, cuts),
        in_specs=[vmem] * 4,
        out_specs=(vmem,) * len(outs),
        out_shape=outs,
        compiler_params=pltpu.CompilerParams(vmem_limit_bytes=VMEM_LIMIT),
        cost_estimate=pl.CostEstimate(
            flops=rows * width * width // 4, bytes_accessed=rows * width // 4, transcendentals=0
        ),
    )(mine, theirs, pin(weight), pin(other))


def cross(piece):
    size = lax.axis_size("ha")
    return [piece] + [flip(piece, "ha", step) for step in range(2, size, 2)]


def swap(piece):
    rows = piece.shape[0] - MOD_ROWS
    cuts = [0] + [MOD_ROWS + rows * n // PARTS for n in range(1, PARTS + 1)]
    return tuple(flip(piece[start:stop], "ha", 1) for start, stop in zip(cuts, cuts[1:]))


def paired(pieces):
    return [shard for piece in pieces for shard in (piece, swap(piece))]


def spread(piece):
    return paired(cross(piece))


def after_all(pieces, other):
    return [pieces[0]] + [after(piece, other) for piece in pieces[1:]]


def after(x, *others):
    return lax.optimization_barrier((x, *others))[0]


def on_device(latents, timesteps, mod_weight, qkv_weight, out_weight, noise_frame):
    frames, tok_count, width = latents.shape
    ha_size, pb_size = lax.axis_size("ha"), lax.axis_size("pb")
    ha, pb = lax.axis_index("ha"), lax.axis_index("pb")
    ids = jnp.stack([ha, pb]).astype(jnp.int32)
    piece = latents.reshape(tok_count, width)
    weight = jnp.transpose(qkv_weight, (1, 0, 2))

    embedding = sinusoid(timesteps).astype(BF16)
    modulation = jnp.einsum(
        "pe,jef->pjf", embedding, jnp.transpose(mod_weight, (1, 0, 2)), preferred_element_type=F32
    ).astype(BF16)
    gate = modulation[:, 2].astype(F32)
    mod_rows = jnp.pad(modulation[0, :2], ((0, MOD_ROWS - 2), (0, 0)))
    carried = jnp.concatenate([mod_rows, piece], axis=0)

    weight, out_local, columns = fetch(after(ids, carried), weight, out_weight, ha_size)

    def frame(pieces, state=None, last=False):
        got = frame_step(ids, pieces, weight, state, last)
        return got[0] if last else got if state is None else (state[0], *got)

    if pb_size == 4:
        pairs, middle, outward = [(0, 1), (1, 0), (2, 3), (3, 2)], [(1, 2), (2, 1)], [(1, 0), (2, 3)]
        own = cross(carried)
        first = after(lax.ppermute(carried, "pb", pairs), weight)
        first_over = cross(first)
        passed = lax.ppermute(first, "pb", middle)
        crossed = after(lax.ppermute(carried, "pb", middle), weight, first)
        beyond = lax.ppermute(crossed, "pb", outward)
        q, k, v = frame(paired(after_all(own, weight)))
        passed = after(passed, q)
        onward = lax.ppermute(passed, "pb", outward)
        second = add(crossed, after(beyond, passed))
        second_over = cross(second)
        state = frame(paired([after(p, passed) for p in first_over]), (q,))
        third = cross(add(passed, after(onward, state[1])))
        state = (q, *own_step(q, k, v, *state[1:]))
        state = frame(paired([after(p, state[1]) for p in second_over]), state)
        rest = paired([after(p, state[1]) for p in third])
        other_weight = flip(after(columns, rest), "ha", 1)
        attended = frame(rest, state, True)
    else:
        other_weight = flip(columns, "ha", 1)
        q, k, v = frame(spread(carried))
        state = (q,)
        for bit in range(1, pb_size):
            state = frame(spread(flip(carried, "pb", bit)), state, bit == pb_size - 1)
            if bit == 1:
                state = (q, *own_step(q, k, v, *state[1:]))
        attended = state

    is_last = (pb == pb_size - 1).astype(jnp.int32).reshape(1)
    done, following = [], []
    cuts = tuple(tok_count * n // 24 for n in (0, 7, 15, 24))
    theirs = flip(attended, "ha", 1)
    sent = []
    for step in range(2, ha_size, 2):
        parts = []
        for at in zip(cuts, cuts[1:]):
            parts += project(after(attended, *parts[-1:]), theirs, out_local, other_weight, step, at, BF16)
        sent.append([flip(part, "ha", step) for part in parts])
    mine = project(attended, theirs, out_local, other_weight, 0, cuts, F32)
    for n, (start, stop, branch) in enumerate(zip(cuts, cuts[1:], mine)):
        others = [after(parts[n], *mine, *done[-1:]) for parts in sent]
        advanced = finish(piece[start:stop], gate, branch, *others)
        done.append(advanced)
        following.append(from_behind(advanced, "pb", -1))
    queue = None
    for n, incoming in enumerate(following):
        queue = place(cuts[n], is_last, incoming if n == 0 else after(incoming, queue), noise_frame, queue)
    return jnp.concatenate(done, axis=0)[None], queue[None]


def solution(mesh):
    placed = (
        P(("grp", "pb"), None, "ha"),
        P(("grp", "pb")),
        P(None, None, "ha"),
        P(None, None, "ha"),
        P("ha", None),
        P("grp", "ha"),
    )
    return jax.shard_map(
        on_device,
        mesh=mesh,
        in_specs=placed,
        out_specs=(P(("grp", "pb"), None, "ha"), P(("grp", "pb"), None, "ha")),
        check_vma=False,
    )
```
